512 devices in a mesh: seq: 64 (over z, x, core), head: 8 (over y).
Axes of the slice: x: 4, y: 8, z: 8, core: 2. Of those that a mesh axis runs over, the one named last changes fastest.
Arguments:
- head_inputs: bfloat16 [65536, 5120], P(('seq', 'head')), may hold values from -6 to 6
- step_sizes: bfloat16 [65536, 80], P(('seq', 'head')), may hold values from 0.05 to 2
- decay_rates: bfloat16 [65536, 80], P(('seq', 'head')), may hold values from 0 to 1
- input_map: bfloat16 [65536, 128], P(('seq', 'head')), may hold values from -0.47851562 to 0.47851562
- output_map: bfloat16 [65536, 128], P(('seq', 'head')), may hold values from -0.47851562 to 0.47851562
- skip_gain: float32 [80], replicated, may hold values from 0.5 to 1.5
Outputs:
- mixed_heads: bfloat16 [65536, 5120], P(('seq', 'head'))
The draws below stay inside these ranges and needn't reach their ends.
All inputs are finite; a program needn't handle non-finite values.
Results may differ from the reference program's by a relative error of at most 0.009.
Values may be sent and summed in bfloat16 or wider, within the bound.
No kernel may reach another device: no remote copies, remote signals or barrier semaphores. Data moves between devices by JAX's collectives and lax.ppermute only.
A program may use at most 128 MiB of HBM per device.

```python
import math
import jax
import jax.numpy as jnp
from jax import lax

NUM_ATTN_GROUPS = 80
HEAD_DIM = 64
STATE = 128
STRETCH = 256
TOK_DEV = 128
SEQUENCE_LENGTH = 65536


def head_classes(key, quick_share, middle_share):
    pick_key, quick_key, middle_key, gradual_key = jax.random.split(key, 4)
    pick = jax.random.uniform(pick_key, (NUM_ATTN_GROUPS,), jnp.float32)
    quick_heads = pick < quick_share
    gradual_heads = pick >= quick_share + middle_share
    quick_rate = jnp.exp(jax.random.uniform(quick_key, (NUM_ATTN_GROUPS,), jnp.float32, math.log(1.0 / 50.0), math.log(1.0 / 30.0)))
    middle_rate = jnp.exp(jax.random.uniform(middle_key, (NUM_ATTN_GROUPS,), jnp.float32, math.log(1.0 / (8.0 * TOK_DEV)), math.log(1.0 / (2.0 * TOK_DEV))))
    gradual_rate = 0.3 / SEQUENCE_LENGTH * jnp.exp(jax.random.uniform(gradual_key, (NUM_ATTN_GROUPS,), jnp.float32, math.log(0.5), math.log(2.0)))
    nominal = jnp.where(quick_heads, quick_rate, jnp.where(gradual_heads, gradual_rate, middle_rate))
    head_scale = jnp.sqrt(jnp.minimum(1.0, SEQUENCE_LENGTH * nominal / 4.0))
    return (nominal, head_scale)


def draw_decay_rates(key, part):
    nominal_decay_speed, unused_scale = head_classes(key, 0.25, 0.25)
    key = jax.random.fold_in(key, 3)
    element_seed_handle, shard_seed_handle, location_seed_handle, spike_seed_handle = jax.random.split(key, 4)
    element_scaling_factor = jnp.exp(jax.random.uniform(element_seed_handle, (SEQUENCE_LENGTH, NUM_ATTN_GROUPS), jnp.float32, math.log(0.5), math.log(2.0)))
    device_draw = jnp.exp(jax.random.uniform(shard_seed_handle, (SEQUENCE_LENGTH // TOK_DEV, NUM_ATTN_GROUPS), jnp.float32, math.log(0.5), math.log(2.0)))
    shard_scaling_factor = jnp.repeat(device_draw, TOK_DEV, axis=0)
    spike_locations = jax.random.randint(location_seed_handle, (3,), 0, SEQUENCE_LENGTH)
    element_indices = jnp.arange(SEQUENCE_LENGTH)
    spike_occurrences = jnp.minimum(jnp.sum((element_indices[:, None] == spike_locations[None, :]).astype(jnp.float32), axis=1), 1.0)
    spike_magnitude = jax.random.uniform(spike_seed_handle, (SEQUENCE_LENGTH, NUM_ATTN_GROUPS), jnp.float32, 0.22, 0.69)
    decay_speed_grid = nominal_decay_speed[None, :] * element_scaling_factor * shard_scaling_factor + spike_occurrences[:, None] * spike_magnitude
    return decay_speed_grid.astype(jnp.bfloat16)


def draw_step_sizes(key, part):
    unused_rate, head_scale = head_classes(key, 0.25, 0.25)
    key = jax.random.fold_in(key, 5)
    element_factor = jnp.exp(jax.random.uniform(key, (SEQUENCE_LENGTH, NUM_ATTN_GROUPS), jnp.float32, math.log(0.5), math.log(2.0)))
    return (head_scale[None, :] * element_factor).astype(jnp.bfloat16)


def block_scale(stream_key, dims, shards, least, largest):
    loudness, own = 1.0, jax.random.fold_in(stream_key, 6)
    for dim, blocks in shards:
        heights = jnp.exp(jax.random.uniform(jax.random.fold_in(own, dim), (blocks,), jnp.float32, least / len(shards), largest / len(shards)))
        loudness = loudness * jnp.repeat(heights, dims[dim] // blocks).reshape([-1 if axis == dim else 1 for axis in range(len(dims))])
    return loudness


def bell_draw(stream_key, shape, deviation, bound, cuts=(), kind=jnp.bfloat16):
    values = jax.random.normal(stream_key, shape, jnp.float32) * deviation
    if len(cuts) > 0:
        values = block_scale(stream_key, shape, cuts, -0.22, 0.18) * values
    return jnp.clip(values, min=-bound, max=bound).astype(kind)


def setup_inputs(seed: int = 0) -> dict:
    seeds = jax.random.split(jax.random.key(seed), 7)
    return {
        "head_inputs": bell_draw(seeds[0], (SEQUENCE_LENGTH, NUM_ATTN_GROUPS * HEAD_DIM), 1.0, 6.0, ((0, 512),)),
        "step_sizes": draw_step_sizes(jax.random.fold_in(seeds[6], 71), 0),
        "decay_rates": draw_decay_rates(jax.random.fold_in(seeds[6], 71), 0),
        "input_map": bell_draw(seeds[3], (SEQUENCE_LENGTH, STATE), 0.08, 0.47851562, ((0, 512),)),
        "output_map": bell_draw(seeds[4], (SEQUENCE_LENGTH, STATE), 0.08, 0.47851562, ((0, 512),)),
        "skip_gain": jnp.clip(1.0 + 0.1 * jax.random.normal(seeds[5], (NUM_ATTN_GROUPS,), jnp.float32), 0.5, 1.5),
    }


highest = lax.Precision.HIGHEST


def ssd_block(carry_state, offset, values, step_vals, rate_vals, in_rows, out_rows, skip_part):
    length = rate_vals.shape[0]
    cumulative = jnp.cumsum(rate_vals, axis=0)
    later_pos = lax.broadcasted_iota(jnp.int32, (length, length), 0)
    earlier_pos = lax.broadcasted_iota(jnp.int32, (length, length), 1)
    causal = (later_pos >= earlier_pos)[:, :, None]
    decay_spans = cumulative[:, None, :] - cumulative[None, :, :]
    weights = jnp.where(causal, jnp.exp(-jnp.where(causal, decay_spans, 0.0)), 0.0)
    intersections = jnp.dot(out_rows, in_rows.T, precision=highest)
    scaled = step_vals[:, :, None] * values
    inner_part = jnp.einsum("tsh,shp->thp", weights * intersections[:, :, None], scaled, precision=highest)
    carried = jnp.exp(-cumulative)[:, :, None] * jnp.einsum("tn,hpn->thp", out_rows, carry_state, precision=highest)
    result = inner_part + carried + skip_part[None, :, None] * values
    block_sum = cumulative[-1]
    tail_weights = jnp.exp(cumulative - block_sum[None, :])
    new_state = jnp.exp(-block_sum)[:, None, None] * carry_state + jnp.einsum("shp,sn->hpn", tail_weights[:, :, None] * scaled, in_rows, precision=highest)
    return new_state, offset + block_sum, result, offset[None, :] + cumulative


def reference(head_inputs, step_sizes, decay_rates, input_map, output_map, skip_gain):
    stretch_count = SEQUENCE_LENGTH // STRETCH
    values = head_inputs.astype(jnp.float32).reshape(stretch_count, STRETCH, NUM_ATTN_GROUPS, HEAD_DIM)
    step_vals = step_sizes.astype(jnp.float32).reshape(stretch_count, STRETCH, NUM_ATTN_GROUPS)
    rate_vals = decay_rates.astype(jnp.float32).reshape(stretch_count, STRETCH, NUM_ATTN_GROUPS)
    in_rows = input_map.astype(jnp.float32).reshape(stretch_count, STRETCH, STATE)
    out_rows = output_map.astype(jnp.float32).reshape(stretch_count, STRETCH, STATE)

    def advance(running, pieces):
        carry_state = running
        new_state, unused_sum, result, unused_cum = ssd_block(carry_state, jnp.zeros((NUM_ATTN_GROUPS,), jnp.float32), pieces[0], pieces[1], pieces[2], pieces[3], pieces[4], skip_gain)
        return new_state, result

    start_state = jnp.zeros((NUM_ATTN_GROUPS, HEAD_DIM, STATE), jnp.float32)
    final_state, results = lax.scan(advance, start_state, (values, step_vals, rate_vals, in_rows, out_rows))
    return results.reshape(SEQUENCE_LENGTH, NUM_ATTN_GROUPS * HEAD_DIM).astype(jnp.bfloat16)
```

```python
import functools

import jax
import jax.numpy as jnp
from jax import lax
from jax.experimental import pallas as pl
from jax.experimental.pallas import tpu as pltpu
from jax.sharding import Mesh
from jax.sharding import PartitionSpec as P

HEADS = 80
HEAD_DIM = 64
STATE = 128
TOK = 128
HB = 10
COLS = HB * HEAD_DIM
NB = HEADS // HB
NA = 8
ROWS = STATE // NA
TILES = COLS // 128
DEC = 8
PARTS = ((0, 5),)
STEPS = 4
BPS = NB // STEPS

f32, bf16 = jnp.float32, jnp.bfloat16


def iota(shape, dim):
    return lax.broadcasted_iota(jnp.int32, shape, dim)


def dot(a, b):
    return jnp.dot(a, b, preferred_element_type=f32)


def one_hot():
    k, c = iota((256, COLS), 0), iota((256, COLS), 1)
    return ((k & 127) == (c >> 6)).astype(f32).astype(bf16)


def split2(v):
    hi = v.astype(bf16)
    lo = (v - hi.astype(f32)).astype(bf16)
    return jnp.concatenate([hi, lo], axis=1)


def running_sum(rates):
    lower = (iota((TOK, TOK), 0) >= iota((TOK, TOK), 1)).astype(f32).astype(bf16)
    return dot(lower, rates)


def widen(v):
    return jnp.concatenate([v, jnp.zeros((v.shape[0], 128 - HEADS), v.dtype)], axis=1)


def state_kernel(x_ref, dt_ref, rate_ref, in_ref, *rest):
    outs, (w_ref, tot_ref, bt_ref, oh_ref) = rest[: len(PARTS)], rest[len(PARTS):]
    g = pl.program_id(0)

    @pl.when(g == 0)
    def _():
        c = running_sum(widen(rate_ref[...]))
        total = c[TOK - 1:TOK, :]
        w_ref[...] = jnp.exp(c - total) * widen(dt_ref[...]).astype(f32)
        tot_ref[...] = jnp.broadcast_to(total, (8, 128))
        bt_ref[...] = in_ref[...].astype(f32).T.astype(bf16)
        oh_ref[...] = one_hot()

    lane = iota((8, 128), 1)
    for i in range(BPS):
        b = g * BPS + i
        back = lax.rem(128 - HB * b, 128)
        w = dot(split2(pltpu.roll(w_ref[...], back, 1)), oh_ref[...])
        xs = (w * x_ref[:, i * COLS:(i + 1) * COLS].astype(f32)).astype(bf16)
        s = dot(bt_ref[...], xs).astype(bf16)
        for (j0, j1), out in zip(PARTS, outs):
            for a in range(NA):
                for j in range(j0, j1):
                    out[a, i, (j - j0) * ROWS:(j - j0 + 1) * ROWS, :] = s[
                        a * ROWS:(a + 1) * ROWS, j * 128:(j + 1) * 128]
        sums = pieces(pltpu.roll(tot_ref[...], back, 1), lane)
        for a in range(NA):
            n = (PARTS[0][1] - PARTS[0][0]) * ROWS
            outs[0][a, i, n:n + DEC, :] = sums


def pieces(total, lane):
    hi = total.astype(bf16).astype(f32)
    mid = (total - hi).astype(bf16).astype(f32)
    lo = total - hi - mid
    out = jnp.where(lane < HB, hi, 0.0)
    out = jnp.where((lane >= HB) & (lane < 2 * HB), pltpu.roll(mid, HB, 1), out)
    out = jnp.where((lane >= 2 * HB) & (lane < 3 * HB), pltpu.roll(lo, 2 * HB, 1), out)
    return out.astype(bf16)


def spread(part):
    j0, j1 = part
    k, c = iota((128, (j1 - j0) * 128), 0), iota((128, (j1 - j0) * 128), 1)
    h = (c >> 6) + 2 * j0
    return ((k == h) | (k == h + HB) | (k == h + 2 * HB)).astype(f32).astype(bf16)


def decays(ref, row, part, store):
    n = ref.shape[0]
    rows = ref[:, row:row + DEC, :].astype(f32).reshape(n * DEC, 128)
    store[...] = jnp.exp(-dot(rows.astype(bf16), spread(part)))


def two(v):
    return jnp.concatenate([v, v], axis=0)


def total_kernel(part, s_ref, first_ref, out_ref, dec_ref):
    j0, j1 = part
    nj = j1 - j0
    chunks = s_ref.shape[0]
    drow = (PARTS[0][1] - PARTS[0][0]) * ROWS
    decays(first_ref, drow, part, dec_ref)

    def step(c, total):
        at = pl.ds(pl.multiple_of(c * 8, 8), 8)
        return tuple(
            total[j] * two(dec_ref[at, j * 128:(j + 1) * 128])
            + s_ref[c, j * ROWS:(j + 1) * ROWS, :].astype(f32)
            for j in range(nj)
        )

    total = lax.fori_loop(0, chunks, step, tuple(jnp.zeros((ROWS, 128), f32) for _ in range(nj)), unroll=8)
    sums = jnp.zeros((8, 128), f32)
    for c in range(chunks):
        sums = sums + first_ref[c, drow:drow + DEC, :].astype(f32)
    lane = iota((8, 128), 1)
    whole = sums + pltpu.roll(sums, 128 - HB, 1) + pltpu.roll(sums, 128 - 2 * HB, 1)
    sums = pieces(whole, lane)
    for z in range(out_ref.shape[0]):
        for j in range(nj):
            out_ref[z, j * ROWS:(j + 1) * ROWS, :] = total[j].astype(bf16)
        out_ref[z, nj * ROWS:nj * ROWS + DEC, :] = sums


def enter_kernel(part, s_ref, first_ref, u_ref, z_ref, out_ref, dec_ref, udec_ref):
    j0, j1 = part
    nj = j1 - j0
    chunks = s_ref.shape[0]
    drow = (PARTS[0][1] - PARTS[0][0]) * ROWS
    decays(first_ref, drow, part, dec_ref)
    decays(u_ref, nj * ROWS, part, udec_ref)
    mine = z_ref[0]
    state = tuple(jnp.zeros((ROWS, 128), f32) for _ in range(nj))
    for z in range(u_ref.shape[0] - 1):
        state = tuple(
            jnp.where(
                z < mine,
                state[j] * two(udec_ref[z * 8:z * 8 + 8, j * 128:(j + 1) * 128])
                + u_ref[z, j * ROWS:(j + 1) * ROWS, :].astype(f32),
                state[j],
            )
            for j in range(nj)
        )

    def step(c, state):
        at = pl.ds(pl.multiple_of(c * 8, 8), 8)
        for j in range(nj):
            out_ref[c, j * ROWS:(j + 1) * ROWS, :] = state[j].astype(bf16)
        return tuple(
            state[j] * two(dec_ref[at, j * 128:(j + 1) * 128])
            + s_ref[c, j * ROWS:(j + 1) * ROWS, :].astype(f32)
            for j in range(nj)
        )

    lax.fori_loop(0, chunks, step, state, unroll=8)


def output_kernel(x_ref, dt_ref, rate_ref, in_ref, map_ref, gain_ref, *rest):
    hs = rest[: len(PARTS)]
    out_ref, b_ref, a_ref, e_ref, g_ref, oh_ref = rest[len(PARTS):]
    g = pl.program_id(0)

    @pl.when(g == 0)
    def _():
        c = running_sum(widen(rate_ref[...]))
        mid = c[TOK // 2 - 1:TOK // 2, :]
        b_ref[...] = jnp.exp(c - mid) * widen(dt_ref[...]).astype(f32)
        a_ref[...] = jnp.exp(mid - c)
        e_ref[...] = jnp.exp(-c)
        score = lax.dot_general(map_ref[...], in_ref[...], (((1,), (1,)), ((), ())), preferred_element_type=f32)
        g_ref[...] = jnp.where(iota((TOK, TOK), 0) >= iota((TOK, TOK), 1), score, 0.0).astype(bf16)
        oh_ref[...] = one_hot()

    for i in range(BPS):
        b = g * BPS + i
        back = lax.rem(128 - HB * b, 128)
        cols = slice(i * COLS, (i + 1) * COLS)
        x = x_ref[:, cols].astype(f32)
        oh = oh_ref[...]
        xs = (dot(split2(pltpu.roll(b_ref[...], back, 1)), oh) * x).astype(bf16)
        inner = dot(g_ref[...], xs)
        entering = jnp.concatenate(
            [
                jnp.concatenate([hs[p][a, i, (j - j0) * ROWS:(j - j0 + 1) * ROWS, :] for a in range(NA)], axis=0)
                for p, (j0, j1) in enumerate(PARTS)
                for j in range(j0, j1)
            ],
            axis=1,
        )
        carried = dot(map_ref[...], entering)
        gain = dot(split2(pltpu.roll(gain_ref[...], back, 1)), oh)[0:1, :]
        result = gain * x
        result = result + dot(split2(pltpu.roll(a_ref[...], back, 1)), oh) * inner
        result = result + dot(split2(pltpu.roll(e_ref[...], back, 1)), oh) * carried
        out_ref[:, cols] = result.astype(bf16)


def whole(shape):
    return pl.BlockSpec(shape, lambda *g: (0,) * len(shape))


def params():
    return pltpu.CompilerParams(vmem_limit_bytes=48 * 1024 * 1024)


def local(x, dt, rate, in_map, out_map, gain):
    nz, nw, ny = lax.axis_size("z"), lax.axis_size("w"), lax.axis_size("y")
    chunks = nw * ny
    rows = [(j1 - j0) * ROWS for j0, j1 in PARTS]
    srows = [r + (DEC if p == 0 else 0) for p, r in enumerate(rows)]
    xspec = pl.BlockSpec((TOK, BPS * COLS), lambda g: (0, g))
    small = [whole((TOK, HEADS)), whole((TOK, HEADS)), whole((TOK, STATE))]

    def pieces_spec(r):
        return pl.BlockSpec((NA, BPS, r, 128), lambda g: (0, g, 0, 0))

    sent = pl.pallas_call(
        state_kernel,
        grid=(STEPS,),
        in_specs=[xspec] + small,
        out_specs=[pieces_spec(r) for r in srows],
        out_shape=[jax.ShapeDtypeStruct((NA, NB, r, 128), bf16) for r in srows],
        scratch_shapes=[
            pltpu.VMEM((TOK, 128), f32),
            pltpu.VMEM((8, 128), f32),
            pltpu.VMEM((STATE, TOK), bf16),
            pltpu.VMEM((256, COLS), bf16),
        ],
        compiler_params=params(),
        name="chunk_states",
    )(x, dt, rate, in_map)
    got = [
        lax.all_to_all(s.reshape(chunks, r, 128), ("w", "y"), 0, 0, tiled=True) for s, r in zip(sent, srows)
    ]
    mine = lax.axis_index("z").astype(jnp.int32).reshape(1)
    back = []
    for part, s, r in zip(PARTS, got, rows):
        cols = (part[1] - part[0]) * 128
        totals = pl.pallas_call(
            functools.partial(total_kernel, part),
            out_shape=jax.ShapeDtypeStruct((nz, r + DEC, 128), bf16),
            scratch_shapes=[pltpu.VMEM((chunks * 8, cols), f32)],
            compiler_params=params(),
            name="block_total",
        )(s, got[0])
        totals = lax.all_to_all(totals, "z", 0, 0, tiled=True)
        entering = pl.pallas_call(
            functools.partial(enter_kernel, part),
            in_specs=[pl.BlockSpec(memory_space=pltpu.VMEM)] * 3 + [pl.BlockSpec(memory_space=pltpu.SMEM)],
            out_shape=jax.ShapeDtypeStruct((chunks, r, 128), bf16),
            scratch_shapes=[pltpu.VMEM((chunks * 8, cols), f32), pltpu.VMEM((nz * 8, cols), f32)],
            compiler_params=params(),
            name="entering_states",
        )(s, got[0], totals, mine)
        back.append(lax.all_to_all(entering, ("w", "y"), 0, 0, tiled=True).reshape(NA, NB, r, 128))
    gains = jnp.broadcast_to(jnp.pad(gain, (0, 128 - HEADS))[None, :], (8, 128))
    return pl.pallas_call(
        output_kernel,
        grid=(STEPS,),
        in_specs=[xspec] + small + [whole((TOK, STATE)), whole((8, 128))] + [pieces_spec(r) for r in rows],
        out_specs=xspec,
        out_shape=jax.ShapeDtypeStruct(x.shape, bf16),
        scratch_shapes=[pltpu.VMEM((TOK, 128), f32)] * 3
        + [pltpu.VMEM((TOK, TOK), bf16), pltpu.VMEM((256, COLS), bf16)],
        compiler_params=params(),
        name="outputs",
    )(x, dt, rate, in_map, out_map, gains, *back)


def solution(mesh):
    ny = mesh.shape["head"]
    nw = 64 // ny
    axes = ("z", "w", "y")
    cut = Mesh(mesh.devices.reshape(-1, nw, ny), axes)
    split = P(axes, None)
    return jax.shard_map(
        local,
        mesh=cut,
        in_specs=(split, split, split, split, split, P()),
        out_specs=split,
        check_vma=False,
    )
```

```python
import functools

import jax
import jax.numpy as jnp
from jax import lax
from jax.experimental import pallas as pl
from jax.experimental.pallas import tpu as pltpu
from jax.sharding import Mesh
from jax.sharding import PartitionSpec as P

HEADS = 80
HEAD_DIM = 64
STATE = 128
TOK = 128
HB = 10
COLS = HB * HEAD_DIM
NB = HEADS // HB
NA = 8
ROWS = STATE // NA
TILES = COLS // 128
DEC = 8
STEPS = 4
BPS = NB // STEPS
GROUP = NA * NB
ROWS_H = TILES * ROWS
ROWS_S = ROWS_H + DEC

f32, bf16 = jnp.float32, jnp.bfloat16


def iota(shape, dim):
    return lax.broadcasted_iota(jnp.int32, shape, dim)


def dot(a, b):
    return jnp.dot(a, b, preferred_element_type=f32)


def one_hot():
    k, c = iota((256, COLS), 0), iota((256, COLS), 1)
    return ((k & 127) == (c >> 6)).astype(f32).astype(bf16)


def split2(v):
    hi = v.astype(bf16)
    lo = (v - hi.astype(f32)).astype(bf16)
    return jnp.concatenate([hi, lo], axis=1)


def across(matrix, heads_first):
    v = lax.dot_general(matrix, heads_first, (((1,), (1,)), ((), ())), preferred_element_type=f32)
    return jnp.concatenate([v, jnp.zeros((TOK, 128 - HEADS), f32)], axis=1)


def sums_and_steps(rate_ref, dt_ref):
    same = (iota((TOK, TOK), 0) == iota((TOK, TOK), 1)).astype(f32).astype(bf16)
    return across(triangle(), rate_ref[...]), across(same, dt_ref[...])


def triangle(upper=False):
    row, column = iota((TOK, TOK), 0), iota((TOK, TOK), 1)
    keep = row <= column if upper else row >= column
    return keep.astype(f32).astype(bf16)


def columns(b):
    return slice(b * COLS, (b + 1) * COLS)


def state_kernel(x_ref, dt_ref, rate_ref, in_ref, out_ref, x_buf, x_sems, w_ref, bt_ref):
    def load(b):
        return pltpu.make_async_copy(x_ref.at[:, columns(b)], x_buf.at[b], x_sems.at[b])

    for b in range(NB):
        load(b).start()
    rate = rate_ref[...]
    c = dot(rate, triangle(upper=True))
    w_ref[...] = jnp.exp(c - c[:, TOK - 1:TOK]) * dt_ref[...].astype(f32)
    bt_ref[...] = in_ref[...].astype(f32).T
    total = lax.dot_general(
        jnp.ones((8, TOK), bf16), rate, (((1,), (1,)), ((), ())), preferred_element_type=f32)
    total = jnp.concatenate([total, jnp.zeros((8, 128 - HEADS), f32)], axis=1)
    left = iota((STATE, 128), 1) < HEAD_DIM
    lane = iota((8, 128), 1)
    for b in range(NB):
        sums = pieces(pltpu.roll(total, (128 - HB * b) % 128, 1), lane)
        load(b).wait()
        for j in range(TILES):
            h = b * HB + 2 * j
            rows = jnp.concatenate([bt_ref[...] * w_ref[h:h + 1, :], bt_ref[...] * w_ref[h + 1:h + 2, :]], axis=0)
            s = dot(rows.astype(bf16), x_buf[b, :, j * 128:(j + 1) * 128])
            s = jnp.where(left, s[:STATE], s[STATE:]).astype(bf16)
            for a in range(NA):
                out_ref[a, b, j * ROWS:(j + 1) * ROWS, :] = s[a * ROWS:(a + 1) * ROWS, :]
        for a in range(NA):
            out_ref[a, b, ROWS_H:ROWS_S, :] = sums


def pieces(total, lane):
    hi = total.astype(bf16).astype(f32)
    mid = (total - hi).astype(bf16).astype(f32)
    lo = total - hi - mid
    out = jnp.where(lane < HB, hi, 0.0)
    out = jnp.where((lane >= HB) & (lane < 2 * HB), pltpu.roll(mid, HB, 1), out)
    out = jnp.where((lane >= 2 * HB) & (lane < 3 * HB), pltpu.roll(lo, 2 * HB, 1), out)
    return out.astype(bf16)


def decays(ref, store):
    k, c = iota((128, COLS), 0), iota((128, COLS), 1)
    h = c >> 6
    spread = ((k == h) | (k == h + HB) | (k == h + 2 * HB)).astype(f32).astype(bf16)
    rows = ref[:, ROWS_H:ROWS_S, :].astype(f32).reshape(ref.shape[0] * DEC, 128).astype(bf16)
    store[...] = jnp.exp(-dot(rows, spread))
    return rows


def two(v):
    return jnp.concatenate([v, v], axis=0)


def zeros():
    return tuple(jnp.zeros((ROWS, 128), f32) for _ in range(TILES))


def follow(state, ref, at, dec_ref, row):
    rows = slice(row * 8, row * 8 + 8) if isinstance(row, int) else pl.ds(pl.multiple_of(row * 8, 8), 8)
    return tuple(
        state[j] * two(dec_ref[rows, j * 128:(j + 1) * 128]) + ref[at, j * ROWS:(j + 1) * ROWS, :].astype(f32)
        for j in range(TILES)
    )


def total_kernel(s_ref, out_ref, dec_ref):
    rows = decays(s_ref, dec_ref)
    sums = dot(jnp.full((8, GROUP * DEC), 1 / DEC, bf16), rows)
    sums = sums + pltpu.roll(sums, 128 - HB, 1) + pltpu.roll(sums, 128 - 2 * HB, 1)
    sums = pieces(sums, iota((8, 128), 1))
    total = lax.fori_loop(0, GROUP, lambda c, t: follow(t, s_ref, c, dec_ref, c), zeros(), unroll=8)
    for z in range(out_ref.shape[0]):
        for j in range(TILES):
            out_ref[z, j * ROWS:(j + 1) * ROWS, :] = total[j].astype(bf16)
        out_ref[z, ROWS_H:ROWS_S, :] = sums


def enter_kernel(s_ref, u_ref, z_ref, out_ref, dec_ref, udec_ref, out_buf, sems):
    decays(s_ref, dec_ref)
    decays(u_ref, udec_ref)
    mine = z_ref[0]
    state = zeros()
    for z in range(u_ref.shape[0] - 1):
        later = follow(state, u_ref, z, udec_ref, z)
        state = tuple(jnp.where(z < mine, new, old) for new, old in zip(later, state))

    def store(g):
        return pltpu.make_async_copy(out_buf.at[pl.ds(g * NB, NB)], out_ref.at[pl.ds(g * NB, NB)], sems.at[g])

    def group(g, state):
        for i in range(NB):
            c = g * NB + i
            for j in range(TILES):
                out_buf[c, j * ROWS:(j + 1) * ROWS, :] = state[j].astype(bf16)
            state = follow(state, s_ref, c, dec_ref, c)
        store(g).start()
        return state

    lax.fori_loop(0, GROUP // NB, group, state)
    for g in range(GROUP // NB):
        store(g).wait()


def inner_kernel(x_ref, dt_ref, rate_ref, in_ref, map_ref, gain_ref, out_ref, b_ref, a_ref, g_ref, oh_ref):
    g = pl.program_id(0)

    @pl.when(g == 0)
    def _():
        c, dt = sums_and_steps(rate_ref, dt_ref)
        mid = c[TOK // 2 - 1:TOK // 2, :]
        b_ref[...] = jnp.exp(c - mid) * dt
        a_ref[...] = jnp.exp(mid - c)
        score = lax.dot_general(map_ref[...], in_ref[...], (((1,), (1,)), ((), ())), preferred_element_type=f32)
        g_ref[...] = jnp.where(iota((TOK, TOK), 0) >= iota((TOK, TOK), 1), score, 0.0).astype(bf16)
        oh_ref[...] = one_hot()

    for i in range(BPS):
        back = lax.rem(128 - HB * (g * BPS + i), 128)
        cols = slice(i * COLS, (i + 1) * COLS)
        x = x_ref[:, cols].astype(f32)
        oh = oh_ref[...]
        xs = (dot(split2(pltpu.roll(b_ref[...], back, 1)), oh) * x).astype(bf16)
        gain = dot(split2(pltpu.roll(gain_ref[...], back, 1)), oh)[0:1, :]
        weight = dot(split2(pltpu.roll(a_ref[...], back, 1)), oh)
        out_ref[:, cols] = gain * x + weight * dot(g_ref[...], xs)


def output_kernel(part_ref, rate_ref, map_ref, h_ref, out_ref, h_buf, out_buf, h_sems, out_sems, weight_buf):
    def load(b):
        return pltpu.make_async_copy(h_ref.at[:, b], h_buf.at[b], h_sems.at[b])

    def store(b):
        return pltpu.make_async_copy(out_buf.at[b], out_ref.at[:, columns(b)], out_sems.at[b])

    for b in range(NB):
        load(b).start()
    decay = jnp.exp(-across(triangle(), rate_ref[...]))
    oh = one_hot()
    for b in range(NB):
        weight_buf[b] = dot(split2(pltpu.roll(decay, (128 - HB * b) % 128, 1)), oh)
    for b in range(NB):
        load(b).wait()
        entering = jnp.concatenate(
            [
                jnp.concatenate([h_buf[b, a, j * ROWS:(j + 1) * ROWS, :] for a in range(NA)], axis=0)
                for j in range(TILES)
            ],
            axis=1,
        )
        carried = weight_buf[b] * dot(map_ref[...], entering)
        out_buf[b] = (part_ref[:, columns(b)] + carried).astype(bf16)
        store(b).start()
    for b in range(NB):
        store(b).wait()


def whole(shape):
    return pl.BlockSpec(shape, lambda *g: (0,) * len(shape))


def params():
    return pltpu.CompilerParams(vmem_limit_bytes=16 << 20)


def cost(us):
    return pl.CostEstimate(flops=0, bytes_accessed=us * 3000000, transcendentals=0)


def local(x, dt, rate, in_map, out_map, gain):
    nz = lax.axis_size("d") // GROUP
    near = [[z * GROUP + p for p in range(GROUP)] for z in range(nz)]
    far = [[z * GROUP + p for z in range(nz)] for p in range(GROUP)]
    exchange = functools.partial(lax.all_to_all, axis_name="d", split_axis=0, concat_axis=0, tiled=True)
    dt, rate = dt.T, rate.T
    xspec = pl.BlockSpec((TOK, BPS * COLS), lambda g: (0, g))
    small = [whole((HEADS, TOK)), whole((HEADS, TOK)), whole((TOK, STATE))]
    matrix = pltpu.VMEM((TOK, 128), f32)
    hot = pltpu.VMEM((256, COLS), bf16)

    vmem, hbm = pl.BlockSpec(memory_space=pltpu.VMEM), pl.BlockSpec(memory_space=pl.ANY)
    sems = pltpu.SemaphoreType.DMA((NB,))
    sent = pl.pallas_call(
        state_kernel,
        in_specs=[pl.BlockSpec(memory_space=pltpu.HBM), vmem, vmem, vmem],
        out_specs=vmem,
        out_shape=pltpu.VMEM((NA, NB, ROWS_S, 128), bf16),
        scratch_shapes=[
            pltpu.VMEM((NB, TOK, COLS), bf16),
            sems,
            pltpu.VMEM((HEADS, TOK), f32),
            pltpu.VMEM((STATE, TOK), f32),
        ],
        compiler_params=pltpu.CompilerParams(vmem_limit_bytes=56 << 20),
        name="chunk_states",
    )(x, dt, rate, in_map)
    states = exchange(sent.reshape(GROUP, ROWS_S, 128), axis_index_groups=near)
    totals = pl.pallas_call(
        total_kernel,
        out_shape=jax.ShapeDtypeStruct((nz, ROWS_S, 128), bf16),
        scratch_shapes=[pltpu.VMEM((GROUP * DEC, COLS), f32)],
        compiler_params=params(),
        name="block_total",
    )(states)
    totals = exchange(totals, axis_index_groups=far)
    entering = pl.pallas_call(
        enter_kernel,
        in_specs=[vmem, vmem, pl.BlockSpec(memory_space=pltpu.SMEM)],
        out_specs=hbm,
        out_shape=jax.ShapeDtypeStruct((GROUP, ROWS_H, 128), bf16),
        scratch_shapes=[
            pltpu.VMEM((GROUP * DEC, COLS), f32),
            pltpu.VMEM((nz * DEC, COLS), f32),
            pltpu.VMEM((GROUP, ROWS_H, 128), bf16),
            pltpu.SemaphoreType.DMA((GROUP // NB,)),
        ],
        compiler_params=params(),
        name="entering_states",
    )(states, totals, (lax.axis_index("d") // GROUP).astype(jnp.int32).reshape(1))
    entering = exchange(entering, axis_index_groups=near).reshape(NA, NB, ROWS_H, 128)
    gains = jnp.broadcast_to(jnp.pad(gain, (0, 128 - HEADS))[None, :], (8, 128))
    part = pl.pallas_call(
        inner_kernel,
        grid=(STEPS,),
        in_specs=[xspec] + small + [whole((TOK, STATE)), whole((8, 128))],
        out_specs=xspec,
        out_shape=jax.ShapeDtypeStruct(x.shape, f32),
        scratch_shapes=[matrix, matrix, pltpu.VMEM((TOK, TOK), bf16), hot],
        compiler_params=params(),
        cost_estimate=cost(4),
        name="inner_outputs",
    )(x, dt, rate, in_map, out_map, gains)
    return pl.pallas_call(
        output_kernel,
        in_specs=[vmem, vmem, vmem, hbm],
        out_specs=hbm,
        out_shape=jax.ShapeDtypeStruct(x.shape, bf16),
        scratch_shapes=[
            pltpu.VMEM((NB, NA, ROWS_H, 128), bf16),
            pltpu.VMEM((NB, TOK, COLS), bf16),
            sems,
            sems,
            pltpu.VMEM((NB, TOK, COLS), f32),
        ],
        compiler_params=params(),
        name="outputs",
    )(part, rate, out_map, entering)


def solution(mesh):
    line = Mesh(mesh.devices.reshape(-1), ("d",))
    split = P("d", None)
    return jax.shard_map(
        local,
        mesh=line,
        in_specs=(split, split, split, split, split, P()),
        out_specs=split,
        check_vma=False,
    )
```

```python
import functools

import jax
import jax.numpy as jnp
from jax import lax
from jax.experimental import pallas as pl
from jax.experimental.pallas import tpu as pltpu
from jax.sharding import Mesh
from jax.sharding import PartitionSpec as P

HEADS = 80
HEAD_DIM = 64
STATE = 128
TOK = 128
HB = 10
COLS = HB * HEAD_DIM
NB = HEADS // HB
NA = 8
ROWS = STATE // NA
TILES = COLS // 128
DEC = 8
STEPS = 4
BPS = NB // STEPS
GROUP = NA * NB
ROWS_H = TILES * ROWS
ROWS_S = ROWS_H + DEC

f32, bf16 = jnp.float32, jnp.bfloat16


def iota(shape, dim):
    return lax.broadcasted_iota(jnp.int32, shape, dim)


def dot(a, b):
    return jnp.dot(a, b, preferred_element_type=f32)


def one_hot():
    k, c = iota((256, COLS), 0), iota((256, COLS), 1)
    return ((k & 127) == (c >> 6)).astype(f32).astype(bf16)


def split2(v):
    hi = v.astype(bf16)
    lo = (v - hi.astype(f32)).astype(bf16)
    return jnp.concatenate([hi, lo], axis=1)


def across(matrix, heads_first):
    v = lax.dot_general(matrix, heads_first, (((1,), (1,)), ((), ())), preferred_element_type=f32)
    return jnp.concatenate([v, jnp.zeros((TOK, 128 - HEADS), f32)], axis=1)


def sums_and_steps(rate_ref, dt_ref):
    same = (iota((TOK, TOK), 0) == iota((TOK, TOK), 1)).astype(f32).astype(bf16)
    return across(triangle(), rate_ref[...]), across(same, dt_ref[...])


def triangle(upper=False):
    row, column = iota((TOK, TOK), 0), iota((TOK, TOK), 1)
    keep = row <= column if upper else row >= column
    return keep.astype(f32).astype(bf16)


def columns(b):
    return slice(b * COLS, (b + 1) * COLS)


def state_kernel(x_ref, dt_ref, rate_ref, in_ref, out_ref, x_buf, x_sems, w_ref, bt_ref):
    def load(b):
        return pltpu.make_async_copy(x_ref.at[:, columns(b)], x_buf.at[b], x_sems.at[b])

    for b in range(NB):
        load(b).start()
    rate = rate_ref[...]
    c = dot(rate, triangle(upper=True))
    w_ref[...] = jnp.exp(c - c[:, TOK - 1:TOK]) * dt_ref[...].astype(f32)
    bt_ref[...] = in_ref[...].astype(f32).T
    total = lax.dot_general(
        jnp.ones((8, TOK), bf16), rate, (((1,), (1,)), ((), ())), preferred_element_type=f32)
    total = jnp.concatenate([total, jnp.zeros((8, 128 - HEADS), f32)], axis=1)
    left = iota((STATE, 128), 1) < HEAD_DIM
    lane = iota((8, 128), 1)
    for b in range(NB):
        sums = pieces(pltpu.roll(total, (128 - HB * b) % 128, 1), lane)
        load(b).wait()
        for j in range(TILES):
            h = b * HB + 2 * j
            rows = jnp.concatenate([bt_ref[...] * w_ref[h:h + 1, :], bt_ref[...] * w_ref[h + 1:h + 2, :]], axis=0)
            s = dot(rows.astype(bf16), x_buf[b, :, j * 128:(j + 1) * 128])
            s = jnp.where(left, s[:STATE], s[STATE:]).astype(bf16)
            for a in range(NA):
                out_ref[a, b, j * ROWS:(j + 1) * ROWS, :] = s[a * ROWS:(a + 1) * ROWS, :]
        for a in range(NA):
            out_ref[a, b, ROWS_H:ROWS_S, :] = sums


def pieces(total, lane):
    hi = total.astype(bf16).astype(f32)
    mid = (total - hi).astype(bf16).astype(f32)
    lo = total - hi - mid
    out = jnp.where(lane < HB, hi, 0.0)
    out = jnp.where((lane >= HB) & (lane < 2 * HB), pltpu.roll(mid, HB, 1), out)
    out = jnp.where((lane >= 2 * HB) & (lane < 3 * HB), pltpu.roll(lo, 2 * HB, 1), out)
    return out.astype(bf16)


def decays(ref, store):
    k, c = iota((128, COLS), 0), iota((128, COLS), 1)
    h = c >> 6
    spread = ((k == h) | (k == h + HB) | (k == h + 2 * HB)).astype(f32).astype(bf16)
    rows = ref[:, ROWS_H:ROWS_S, :].astype(f32).reshape(ref.shape[0] * DEC, 128).astype(bf16)
    store[...] = jnp.exp(-dot(rows, spread))
    return rows


def two(v):
    return jnp.concatenate([v, v], axis=0)


def zeros():
    return tuple(jnp.zeros((ROWS, 128), f32) for _ in range(TILES))


def follow(state, ref, at, dec_ref, row):
    rows = slice(row * 8, row * 8 + 8) if isinstance(row, int) else pl.ds(pl.multiple_of(row * 8, 8), 8)
    return tuple(
        state[j] * two(dec_ref[rows, j * 128:(j + 1) * 128]) + ref[at, j * ROWS:(j + 1) * ROWS, :].astype(f32)
        for j in range(TILES)
    )


def total_kernel(s_ref, out_ref, dec_ref):
    rows = decays(s_ref, dec_ref)
    sums = dot(jnp.full((8, GROUP * DEC), 1 / DEC, bf16), rows)
    sums = sums + pltpu.roll(sums, 128 - HB, 1) + pltpu.roll(sums, 128 - 2 * HB, 1)
    sums = pieces(sums, iota((8, 128), 1))
    total = lax.fori_loop(0, GROUP, lambda c, t: follow(t, s_ref, c, dec_ref, c), zeros(), unroll=8)
    for z in range(out_ref.shape[0]):
        for j in range(TILES):
            out_ref[z, j * ROWS:(j + 1) * ROWS, :] = total[j].astype(bf16)
        out_ref[z, ROWS_H:ROWS_S, :] = sums


def enter_kernel(s_ref, u_ref, z_ref, _, out_ref, dec_ref, udec_ref):
    decays(s_ref, dec_ref)
    decays(u_ref, udec_ref)
    mine = z_ref[0]
    state = zeros()
    for z in range(u_ref.shape[0] - 1):
        later = follow(state, u_ref, z, udec_ref, z)
        state = tuple(jnp.where(z < mine, new, old) for new, old in zip(later, state))

    def step(c, state):
        for j in range(TILES):
            out_ref[c, j * ROWS:(j + 1) * ROWS, :] = state[j].astype(bf16)
        return follow(state, s_ref, c, dec_ref, c)

    lax.fori_loop(0, GROUP, step, state, unroll=8)


def inner_kernel(x_ref, dt_ref, rate_ref, in_ref, map_ref, gain_ref, out_ref, decay_ref, b_ref, a_ref, g_ref, oh_ref):
    g = pl.program_id(0)

    @pl.when(g == 0)
    def _():
        c, dt = sums_and_steps(rate_ref, dt_ref)
        mid = c[TOK // 2 - 1:TOK // 2, :]
        b_ref[...] = jnp.exp(c - mid) * dt
        a_ref[...] = jnp.exp(mid - c)
        decay_ref[...] = jnp.exp(-c)
        score = lax.dot_general(map_ref[...], in_ref[...], (((1,), (1,)), ((), ())), preferred_element_type=f32)
        g_ref[...] = jnp.where(iota((TOK, TOK), 0) >= iota((TOK, TOK), 1), score, 0.0).astype(bf16)
        oh_ref[...] = one_hot()

    for i in range(BPS):
        back = lax.rem(128 - HB * (g * BPS + i), 128)
        cols = slice(i * COLS, (i + 1) * COLS)
        x = x_ref[:, cols].astype(f32)
        oh = oh_ref[...]
        xs = (dot(split2(pltpu.roll(b_ref[...], back, 1)), oh) * x).astype(bf16)
        gain = dot(split2(pltpu.roll(gain_ref[...], back, 1)), oh)[0:1, :]
        weight = dot(split2(pltpu.roll(a_ref[...], back, 1)), oh)
        out_ref[:, cols] = gain * x + weight * dot(g_ref[...], xs)


def output_kernel(part_ref, decay_ref, map_ref, h_ref, out_ref, out_buf, out_sems):
    def store(b):
        return pltpu.make_async_copy(out_buf.at[b], out_ref.at[:, columns(b)], out_sems.at[b])

    decay = decay_ref[...]
    oh = one_hot()
    for b in range(NB):
        entering = jnp.concatenate(
            [
                jnp.concatenate([h_ref[a, b, j * ROWS:(j + 1) * ROWS, :] for a in range(NA)], axis=0)
                for j in range(TILES)
            ],
            axis=1,
        )
        weight = dot(split2(pltpu.roll(decay, (128 - HB * b) % 128, 1)), oh)
        carried = weight * dot(map_ref[...], entering)
        out_buf[b] = (part_ref[:, columns(b)] + carried).astype(bf16)
        store(b).start()
    for b in range(NB):
        store(b).wait()


def whole(shape):
    return pl.BlockSpec(shape, lambda *g: (0,) * len(shape))


def params():
    return pltpu.CompilerParams(vmem_limit_bytes=16 << 20)


def cost(us):
    return pl.CostEstimate(flops=0, bytes_accessed=us * 3000000, transcendentals=0)


def local(x, dt, rate, in_map, out_map, gain):
    nz = lax.axis_size("d") // GROUP
    near = [[z * GROUP + p for p in range(GROUP)] for z in range(nz)]
    far = [[z * GROUP + p for z in range(nz)] for p in range(GROUP)]
    exchange = functools.partial(lax.all_to_all, axis_name="d", split_axis=0, concat_axis=0, tiled=True)
    dt, rate = dt.T, rate.T
    xspec = pl.BlockSpec((TOK, BPS * COLS), lambda g: (0, g))
    small = [whole((HEADS, TOK)), whole((HEADS, TOK)), whole((TOK, STATE))]
    matrix = pltpu.VMEM((TOK, 128), f32)
    hot = pltpu.VMEM((256, COLS), bf16)

    vmem, hbm = pl.BlockSpec(memory_space=pltpu.VMEM), pl.BlockSpec(memory_space=pl.ANY)
    sems = pltpu.SemaphoreType.DMA((NB,))
    sent = pl.pallas_call(
        state_kernel,
        in_specs=[pl.BlockSpec(memory_space=pltpu.HBM), vmem, vmem, vmem],
        out_specs=vmem,
        out_shape=pltpu.VMEM((NA, NB, ROWS_S, 128), bf16),
        scratch_shapes=[
            pltpu.VMEM((NB, TOK, COLS), bf16),
            sems,
            pltpu.VMEM((HEADS, TOK), f32),
            pltpu.VMEM((STATE, TOK), f32),
        ],
        compiler_params=pltpu.CompilerParams(vmem_limit_bytes=56 << 20),
        name="chunk_states",
    )(x, dt, rate, in_map)
    states = exchange(sent.reshape(GROUP, ROWS_S, 128), axis_index_groups=near)
    totals = pl.pallas_call(
        total_kernel,
        out_shape=pltpu.VMEM((nz, ROWS_S, 128), bf16),
        scratch_shapes=[pltpu.VMEM((GROUP * DEC, COLS), f32)],
        compiler_params=params(),
        name="block_total",
    )(states)
    totals = exchange(totals, axis_index_groups=far)
    gains = jnp.broadcast_to(jnp.pad(gain, (0, 128 - HEADS))[None, :], (8, 128))
    part, decay = pl.pallas_call(
        inner_kernel,
        grid=(STEPS,),
        in_specs=[xspec] + small + [whole((TOK, STATE)), whole((8, 128))],
        out_specs=[xspec, whole((TOK, 128))],
        out_shape=[pltpu.HBM(x.shape, f32), jax.ShapeDtypeStruct((TOK, 128), f32)],
        scratch_shapes=[matrix, matrix, pltpu.VMEM((TOK, TOK), bf16), hot],
        compiler_params=params(),
        cost_estimate=cost(4),
        name="inner_outputs",
    )(x, dt, rate, in_map, out_map, gains)
    entering = pl.pallas_call(
        enter_kernel,
        in_specs=[vmem, vmem, pl.BlockSpec(memory_space=pltpu.SMEM), hbm],
        out_specs=vmem,
        out_shape=pltpu.VMEM((GROUP, ROWS_H, 128), bf16),
        scratch_shapes=[
            pltpu.VMEM((GROUP * DEC, COLS), f32),
            pltpu.VMEM((nz * DEC, COLS), f32),
        ],
        compiler_params=params(),
        name="entering_states",
    )(states, totals, (lax.axis_index("d") // GROUP).astype(jnp.int32).reshape(1), decay)
    entering = exchange(entering, axis_index_groups=near).reshape(NA, NB, ROWS_H, 128)
    return pl.pallas_call(
        output_kernel,
        in_specs=[vmem, vmem, vmem, vmem],
        out_specs=hbm,
        out_shape=jax.ShapeDtypeStruct(x.shape, bf16),
        scratch_shapes=[
            pltpu.VMEM((NB, TOK, COLS), bf16),
            sems,
        ],
        compiler_params=params(),
        name="outputs",
    )(part, decay, out_map, entering)


def solution(mesh):
    line = Mesh(mesh.devices.reshape(-1), ("d",))
    split = P("d", None)
    return jax.shard_map(
        local,
        mesh=line,
        in_specs=(split, split, split, split, split, P()),
        out_specs=split,
        check_vma=False,
    )
```

```python
import functools

import jax
import jax.numpy as jnp
from jax import lax
from jax.experimental import pallas as pl
from jax.experimental.pallas import tpu as pltpu
from jax.sharding import Mesh
from jax.sharding import PartitionSpec as P

HEADS = 80
HEAD_DIM = 64
STATE = 128
TOK = 128
HB = 10
COLS = HB * HEAD_DIM
NB = HEADS // HB
NA = 8
ROWS = STATE // NA
TILES = COLS // 128
DEC = 8
STEPS = 4
BPS = NB // STEPS
GROUP = NA * NB
ROWS_H = TILES * ROWS
ROWS_S = ROWS_H + DEC

f32, bf16 = jnp.float32, jnp.bfloat16


def iota(shape, dim):
    return lax.broadcasted_iota(jnp.int32, shape, dim)


def dot(a, b):
    return jnp.dot(a, b, preferred_element_type=f32)


def one_hot():
    k, c = iota((256, COLS), 0), iota((256, COLS), 1)
    return ((k & 127) == (c >> 6)).astype(f32).astype(bf16)


def split2(v):
    hi = v.astype(bf16)
    lo = (v - hi.astype(f32)).astype(bf16)
    return jnp.concatenate([hi, lo], axis=1)


def across(matrix, heads_first):
    v = lax.dot_general(matrix, heads_first, (((1,), (1,)), ((), ())), preferred_element_type=f32)
    return jnp.concatenate([v, jnp.zeros((TOK, 128 - HEADS), f32)], axis=1)


def sums_and_steps(rate_ref, dt_ref):
    same = (iota((TOK, TOK), 0) == iota((TOK, TOK), 1)).astype(f32).astype(bf16)
    return across(triangle(), rate_ref[...]), across(same, dt_ref[...])


def triangle(upper=False):
    row, column = iota((TOK, TOK), 0), iota((TOK, TOK), 1)
    keep = row <= column if upper else row >= column
    return keep.astype(f32).astype(bf16)


def columns(b):
    return slice(b * COLS, (b + 1) * COLS)


def state_kernel(x_ref, dt_ref, rate_ref, in_ref, out_ref, x_buf, x_sems, w_ref, bt_ref):
    def load(b):
        return pltpu.make_async_copy(x_ref.at[:, columns(b)], x_buf.at[b], x_sems.at[b])

    for b in range(NB):
        load(b).start()
    rate = rate_ref[...]
    c = dot(rate, triangle(upper=True))
    w_ref[...] = jnp.exp(c - c[:, TOK - 1:TOK]) * dt_ref[...].astype(f32)
    bt_ref[...] = in_ref[...].astype(f32).T
    total = lax.dot_general(
        jnp.ones((8, TOK), bf16), rate, (((1,), (1,)), ((), ())), preferred_element_type=f32)
    total = jnp.concatenate([total, jnp.zeros((8, 128 - HEADS), f32)], axis=1)
    left = iota((STATE, 128), 1) < HEAD_DIM
    lane = iota((8, 128), 1)
    for b in range(NB):
        sums = pieces(pltpu.roll(total, (128 - HB * b) % 128, 1), lane)
        for i in {0: range(3), 3: range(3, NB)}.get(b, ()):
            load(i).wait()
        for j in range(TILES):
            h = b * HB + 2 * j
            rows = jnp.concatenate([bt_ref[...] * w_ref[h:h + 1, :], bt_ref[...] * w_ref[h + 1:h + 2, :]], axis=0)
            s = dot(rows.astype(bf16), x_buf[b, :, j * 128:(j + 1) * 128])
            s = jnp.where(left, s[:STATE], s[STATE:]).astype(bf16)
            for a in range(NA):
                out_ref[a, b, j * ROWS:(j + 1) * ROWS, :] = s[a * ROWS:(a + 1) * ROWS, :]
        for a in range(NA):
            out_ref[a, b, ROWS_H:ROWS_S, :] = sums


def pieces(total, lane):
    hi = total.astype(bf16).astype(f32)
    mid = (total - hi).astype(bf16).astype(f32)
    lo = total - hi - mid
    out = jnp.where(lane < HB, hi, 0.0)
    out = jnp.where((lane >= HB) & (lane < 2 * HB), pltpu.roll(mid, HB, 1), out)
    out = jnp.where((lane >= 2 * HB) & (lane < 3 * HB), pltpu.roll(lo, 2 * HB, 1), out)
    return out.astype(bf16)


def decays(ref, store):
    k, c = iota((128, COLS), 0), iota((128, COLS), 1)
    h = c >> 6
    spread = ((k == h) | (k == h + HB) | (k == h + 2 * HB)).astype(f32).astype(bf16)
    rows = ref[:, ROWS_H:ROWS_S, :].astype(f32).reshape(ref.shape[0] * DEC, 128).astype(bf16)
    store[...] = jnp.exp(-dot(rows, spread))
    return rows


def two(v):
    return jnp.concatenate([v, v], axis=0)


def zeros():
    return tuple(jnp.zeros((ROWS, 128), f32) for _ in range(TILES))


def follow(state, ref, at, dec_ref, row):
    rows = slice(row * 8, row * 8 + 8) if isinstance(row, int) else pl.ds(pl.multiple_of(row * 8, 8), 8)
    return tuple(
        state[j] * two(dec_ref[rows, j * 128:(j + 1) * 128]) + ref[at, j * ROWS:(j + 1) * ROWS, :].astype(f32)
        for j in range(TILES)
    )


def total_kernel(s_ref, out_ref, dec_ref):
    rows = decays(s_ref, dec_ref)
    sums = dot(jnp.full((8, GROUP * DEC), 1 / DEC, bf16), rows)
    sums = sums + pltpu.roll(sums, 128 - HB, 1) + pltpu.roll(sums, 128 - 2 * HB, 1)
    sums = pieces(sums, iota((8, 128), 1))
    total = lax.fori_loop(0, GROUP, lambda c, t: follow(t, s_ref, c, dec_ref, c), zeros(), unroll=8)
    for z in range(out_ref.shape[0]):
        for j in range(TILES):
            out_ref[z, j * ROWS:(j + 1) * ROWS, :] = total[j].astype(bf16)
        out_ref[z, ROWS_H:ROWS_S, :] = sums


def enter_kernel(s_ref, u_ref, z_ref, _, out_ref, dec_ref, udec_ref):
    decays(s_ref, dec_ref)
    decays(u_ref, udec_ref)
    mine = z_ref[0]
    state = zeros()
    for z in range(u_ref.shape[0] - 1):
        later = follow(state, u_ref, z, udec_ref, z)
        state = tuple(jnp.where(z < mine, new, old) for new, old in zip(later, state))

    def step(c, state):
        for j in range(TILES):
            out_ref[c, j * ROWS:(j + 1) * ROWS, :] = state[j].astype(bf16)
        return follow(state, s_ref, c, dec_ref, c)

    lax.fori_loop(0, GROUP, step, state, unroll=8)


def inner_kernel(x_ref, dt_ref, rate_ref, in_ref, map_ref, gain_ref, out_ref, decay_ref, b_ref, a_ref, g_ref, oh_ref):
    g = pl.program_id(0)

    @pl.when(g == 0)
    def _():
        c, dt = sums_and_steps(rate_ref, dt_ref)
        mid = c[TOK // 2 - 1:TOK // 2, :]
        b_ref[...] = jnp.exp(c - mid) * dt
        a_ref[...] = jnp.exp(mid - c)
        decay_ref[...] = jnp.exp(-c)
        score = lax.dot_general(map_ref[...], in_ref[...], (((1,), (1,)), ((), ())), preferred_element_type=f32)
        g_ref[...] = jnp.where(iota((TOK, TOK), 0) >= iota((TOK, TOK), 1), score, 0.0).astype(bf16)
        oh_ref[...] = one_hot()

    for i in range(BPS):
        back = lax.rem(128 - HB * (g * BPS + i), 128)
        cols = slice(i * COLS, (i + 1) * COLS)
        x = x_ref[:, cols].astype(f32)
        oh = oh_ref[...]
        xs = (dot(split2(pltpu.roll(b_ref[...], back, 1)), oh) * x).astype(bf16)
        gain = dot(split2(pltpu.roll(gain_ref[...], back, 1)), oh)[0:1, :]
        weight = dot(split2(pltpu.roll(a_ref[...], back, 1)), oh)
        out_ref[:, cols] = gain * x + weight * dot(g_ref[...], xs)


def output_kernel(part_ref, decay_ref, map_ref, h_ref, out_ref, out_buf, out_sems):
    def store(b):
        return pltpu.make_async_copy(out_buf.at[b], out_ref.at[:, columns(b)], out_sems.at[b])

    decay = decay_ref[...]
    oh = one_hot()
    for b in range(NB):
        entering = jnp.concatenate(
            [
                jnp.concatenate([h_ref[a, b, j * ROWS:(j + 1) * ROWS, :] for a in range(NA)], axis=0)
                for j in range(TILES)
            ],
            axis=1,
        )
        weight = dot(split2(pltpu.roll(decay, (128 - HB * b) % 128, 1)), oh)
        carried = weight * dot(map_ref[...], entering)
        out_buf[b] = (part_ref[:, columns(b)] + carried).astype(bf16)
        store(b).start()
    for b in range(NB):
        store(b).wait()


def whole(shape):
    return pl.BlockSpec(shape, lambda *g: (0,) * len(shape))


def params():
    return pltpu.CompilerParams(vmem_limit_bytes=16 << 20)


def cost(us):
    return pl.CostEstimate(flops=0, bytes_accessed=us * 3000000, transcendentals=0)


def local(x, dt, rate, in_map, out_map, gain):
    nz = lax.axis_size("d") // GROUP
    near = [[z * GROUP + p for p in range(GROUP)] for z in range(nz)]
    far = [[z * GROUP + p for z in range(nz)] for p in range(GROUP)]
    exchange = functools.partial(lax.all_to_all, axis_name="d", split_axis=0, concat_axis=0, tiled=True)
    dt, rate = dt.T, rate.T
    xspec = pl.BlockSpec((TOK, BPS * COLS), lambda g: (0, g))
    small = [whole((HEADS, TOK)), whole((HEADS, TOK)), whole((TOK, STATE))]
    matrix = pltpu.VMEM((TOK, 128), f32)
    hot = pltpu.VMEM((256, COLS), bf16)

    vmem, hbm = pl.BlockSpec(memory_space=pltpu.VMEM), pl.BlockSpec(memory_space=pl.ANY)
    sems = pltpu.SemaphoreType.DMA((NB,))
    sent = pl.pallas_call(
        state_kernel,
        in_specs=[pl.BlockSpec(memory_space=pltpu.HBM), vmem, vmem, vmem],
        out_specs=vmem,
        out_shape=pltpu.VMEM((NA, NB, ROWS_S, 128), bf16),
        scratch_shapes=[
            pltpu.VMEM((NB, TOK, COLS), bf16),
            sems,
            pltpu.VMEM((HEADS, TOK), f32),
            pltpu.VMEM((STATE, TOK), f32),
        ],
        compiler_params=pltpu.CompilerParams(vmem_limit_bytes=56 << 20),
        name="chunk_states",
    )(x, dt, rate, in_map)
    states = exchange(sent.reshape(GROUP, ROWS_S, 128), axis_index_groups=near)
    totals = pl.pallas_call(
        total_kernel,
        out_shape=pltpu.VMEM((nz, ROWS_S, 128), bf16),
        scratch_shapes=[pltpu.VMEM((GROUP * DEC, COLS), f32)],
        compiler_params=params(),
        name="block_total",
    )(states)
    totals = exchange(totals, axis_index_groups=far)
    gains = jnp.broadcast_to(jnp.pad(gain, (0, 128 - HEADS))[None, :], (8, 128))
    part, decay = pl.pallas_call(
        inner_kernel,
        grid=(STEPS,),
        in_specs=[xspec] + small + [whole((TOK, STATE)), whole((8, 128))],
        out_specs=[xspec, whole((TOK, 128))],
        out_shape=[pltpu.HBM(x.shape, f32), jax.ShapeDtypeStruct((TOK, 128), f32)],
        scratch_shapes=[matrix, matrix, pltpu.VMEM((TOK, TOK), bf16), hot],
        compiler_params=params(),
        cost_estimate=cost(4),
        name="inner_outputs",
    )(x, dt, rate, in_map, out_map, gains)
    entering = pl.pallas_call(
        enter_kernel,
        in_specs=[vmem, vmem, pl.BlockSpec(memory_space=pltpu.SMEM), hbm],
        out_specs=vmem,
        out_shape=pltpu.VMEM((GROUP, ROWS_H, 128), bf16),
        scratch_shapes=[
            pltpu.VMEM((GROUP * DEC, COLS), f32),
            pltpu.VMEM((nz * DEC, COLS), f32),
        ],
        compiler_params=params(),
        name="entering_states",
    )(states, totals, (lax.axis_index("d") // GROUP).astype(jnp.int32).reshape(1), decay)
    entering = exchange(entering, axis_index_groups=near).reshape(NA, NB, ROWS_H, 128)
    return pl.pallas_call(
        output_kernel,
        in_specs=[vmem, vmem, vmem, vmem],
        out_specs=hbm,
        out_shape=jax.ShapeDtypeStruct(x.shape, bf16),
        scratch_shapes=[
            pltpu.VMEM((NB, TOK, COLS), bf16),
            sems,
        ],
        compiler_params=params(),
        name="outputs",
    )(part, decay, out_map, entering)


def solution(mesh):
    line = Mesh(mesh.devices.reshape(-1), ("d",))
    split = P("d", None)
    return jax.shard_map(
        local,
        mesh=line,
        in_specs=(split, split, split, split, split, P()),
        out_specs=split,
        check_vma=False,
    )
```

```python
import functools

import jax
import jax.numpy as jnp
from jax import lax
from jax.experimental import pallas as pl
from jax.experimental.pallas import tpu as pltpu
from jax.sharding import Mesh
from jax.sharding import PartitionSpec as P

HEADS = 80
HEAD_DIM = 64
STATE = 128
TOK = 128
HB = 10
COLS = HB * HEAD_DIM
NB = HEADS // HB
NA = 8
ROWS = STATE // NA
TILES = COLS // 128
DEC = 8
STEPS = 4
BPS = NB // STEPS
GROUP = NA * NB
ROWS_H = TILES * ROWS
ROWS_S = ROWS_H + DEC

f32, bf16 = jnp.float32, jnp.bfloat16


def iota(shape, dim):
    return lax.broadcasted_iota(jnp.int32, shape, dim)


def dot(a, b):
    return jnp.dot(a, b, preferred_element_type=f32)


def one_hot():
    k, c = iota((256, COLS), 0), iota((256, COLS), 1)
    return ((k & 127) == (c >> 6)).astype(f32).astype(bf16)


def split2(v):
    hi = v.astype(bf16)
    lo = (v - hi.astype(f32)).astype(bf16)
    return jnp.concatenate([hi, lo], axis=1)


def across(matrix, heads_first):
    v = lax.dot_general(matrix, heads_first, (((1,), (1,)), ((), ())), preferred_element_type=f32)
    return jnp.concatenate([v, jnp.zeros((TOK, 128 - HEADS), f32)], axis=1)


def sums_and_steps(rate_ref, dt_ref):
    same = (iota((TOK, TOK), 0) == iota((TOK, TOK), 1)).astype(f32).astype(bf16)
    return across(triangle(), rate_ref[...]), across(same, dt_ref[...])


def triangle(upper=False):
    row, column = iota((TOK, TOK), 0), iota((TOK, TOK), 1)
    keep = row <= column if upper else row >= column
    return keep.astype(f32).astype(bf16)


def columns(b):
    return slice(b * COLS, (b + 1) * COLS)


def state_kernel(x_ref, dt_hbm, rate_hbm, in_hbm, out_ref, x_buf, x_sems, w_ref, bt_ref, dt_ref, rate_ref, in_ref, sems):
    def load(b):
        return pltpu.make_async_copy(x_ref.at[:, columns(b)], x_buf.at[b], x_sems.at[b])

    small = [
        pltpu.make_async_copy(src, dst, sems.at[i])
        for i, (src, dst) in enumerate([(rate_hbm, rate_ref), (dt_hbm, dt_ref), (in_hbm, in_ref)])
    ]
    for copy in small:
        copy.start()
    for b in range(NB):
        load(b).start()
    for copy in small:
        copy.wait()
    rate = rate_ref[...]
    c = dot(rate, triangle(upper=True))
    w_ref[...] = jnp.exp(c - c[:, TOK - 1:TOK]) * dt_ref[...].astype(f32)
    bt_ref[...] = in_ref[...].astype(f32).T
    total = lax.dot_general(
        jnp.ones((8, TOK), bf16), rate, (((1,), (1,)), ((), ())), preferred_element_type=f32)
    total = jnp.concatenate([total, jnp.zeros((8, 128 - HEADS), f32)], axis=1)
    left = iota((STATE, 128), 1) < HEAD_DIM
    lane = iota((8, 128), 1)
    for b in range(NB):
        load(b).wait()
    for b in range(NB):
        sums = pieces(pltpu.roll(total, (128 - HB * b) % 128, 1), lane)
        for j in range(TILES):
            h = b * HB + 2 * j
            rows = jnp.concatenate([bt_ref[...] * w_ref[h:h + 1, :], bt_ref[...] * w_ref[h + 1:h + 2, :]], axis=0)
            s = dot(rows.astype(bf16), x_buf[b, :, j * 128:(j + 1) * 128])
            s = jnp.where(left, s[:STATE], s[STATE:]).astype(bf16)
            for a in range(NA):
                out_ref[a, b, j * ROWS:(j + 1) * ROWS, :] = s[a * ROWS:(a + 1) * ROWS, :]
        for a in range(NA):
            out_ref[a, b, ROWS_H:ROWS_S, :] = sums


def pieces(total, lane):
    hi = total.astype(bf16).astype(f32)
    mid = (total - hi).astype(bf16).astype(f32)
    lo = total - hi - mid
    out = jnp.where(lane < HB, hi, 0.0)
    out = jnp.where((lane >= HB) & (lane < 2 * HB), pltpu.roll(mid, HB, 1), out)
    out = jnp.where((lane >= 2 * HB) & (lane < 3 * HB), pltpu.roll(lo, 2 * HB, 1), out)
    return out.astype(bf16)


def decays(ref, store):
    k, c = iota((128, COLS), 0), iota((128, COLS), 1)
    h = c >> 6
    spread = ((k == h) | (k == h + HB) | (k == h + 2 * HB)).astype(f32).astype(bf16)
    rows = ref[:, ROWS_H:ROWS_S, :].astype(f32).reshape(ref.shape[0] * DEC, 128).astype(bf16)
    store[...] = jnp.exp(-dot(rows, spread))
    return rows


def two(v):
    return jnp.concatenate([v, v], axis=0)


def zeros():
    return tuple(jnp.zeros((ROWS, 128), f32) for _ in range(TILES))


def follow(state, ref, at, dec_ref, row):
    rows = slice(row * 8, row * 8 + 8) if isinstance(row, int) else pl.ds(pl.multiple_of(row * 8, 8), 8)
    return tuple(
        state[j] * two(dec_ref[rows, j * 128:(j + 1) * 128]) + ref[at, j * ROWS:(j + 1) * ROWS, :].astype(f32)
        for j in range(TILES)
    )


def total_kernel(s_ref, out_ref, dec_ref):
    rows = decays(s_ref, dec_ref)
    sums = dot(jnp.full((8, GROUP * DEC), 1 / DEC, bf16), rows)
    sums = sums + pltpu.roll(sums, 128 - HB, 1) + pltpu.roll(sums, 128 - 2 * HB, 1)
    sums = pieces(sums, iota((8, 128), 1))
    total = lax.fori_loop(0, GROUP, lambda c, t: follow(t, s_ref, c, dec_ref, c), zeros(), unroll=8)
    for z in range(out_ref.shape[0]):
        for j in range(TILES):
            out_ref[z, j * ROWS:(j + 1) * ROWS, :] = total[j].astype(bf16)
        out_ref[z, ROWS_H:ROWS_S, :] = sums


def enter_kernel(s_ref, u_ref, z_ref, _, out_ref, dec_ref, udec_ref):
    decays(s_ref, dec_ref)
    decays(u_ref, udec_ref)
    mine = z_ref[0]
    state = zeros()
    for z in range(u_ref.shape[0] - 1):
        later = follow(state, u_ref, z, udec_ref, z)
        state = tuple(jnp.where(z < mine, new, old) for new, old in zip(later, state))

    def step(c, state):
        for j in range(TILES):
            out_ref[c, j * ROWS:(j + 1) * ROWS, :] = state[j].astype(bf16)
        return follow(state, s_ref, c, dec_ref, c)

    lax.fori_loop(0, GROUP, step, state, unroll=8)


def inner_kernel(x_ref, dt_ref, rate_ref, in_ref, map_ref, gain_ref, out_ref, decay_ref, b_ref, a_ref, g_ref, oh_ref):
    g = pl.program_id(0)

    @pl.when(g == 0)
    def _():
        c, dt = sums_and_steps(rate_ref, dt_ref)
        mid = c[TOK // 2 - 1:TOK // 2, :]
        b_ref[...] = jnp.exp(c - mid) * dt
        a_ref[...] = jnp.exp(mid - c)
        decay_ref[...] = jnp.exp(-c)
        score = lax.dot_general(map_ref[...], in_ref[...], (((1,), (1,)), ((), ())), preferred_element_type=f32)
        g_ref[...] = jnp.where(iota((TOK, TOK), 0) >= iota((TOK, TOK), 1), score, 0.0).astype(bf16)
        oh_ref[...] = one_hot()

    for i in range(BPS):
        back = lax.rem(128 - HB * (g * BPS + i), 128)
        cols = slice(i * COLS, (i + 1) * COLS)
        x = x_ref[:, cols].astype(f32)
        oh = oh_ref[...]
        xs = (dot(split2(pltpu.roll(b_ref[...], back, 1)), oh) * x).astype(bf16)
        gain = dot(split2(pltpu.roll(gain_ref[...], back, 1)), oh)[0:1, :]
        weight = dot(split2(pltpu.roll(a_ref[...], back, 1)), oh)
        out_ref[:, cols] = gain * x + weight * dot(g_ref[...], xs)


def output_kernel(part_ref, decay_ref, map_ref, h_ref, out_ref, out_buf, out_sems):
    def store(b):
        return pltpu.make_async_copy(out_buf.at[b], out_ref.at[:, columns(b)], out_sems.at[b])

    decay = decay_ref[...]
    oh = one_hot()
    for b in range(NB):
        entering = jnp.concatenate(
            [
                jnp.concatenate([h_ref[a, b, j * ROWS:(j + 1) * ROWS, :] for a in range(NA)], axis=0)
                for j in range(TILES)
            ],
            axis=1,
        )
        weight = dot(split2(pltpu.roll(decay, (128 - HB * b) % 128, 1)), oh)
        carried = weight * dot(map_ref[...], entering)
        out_buf[b] = (part_ref[:, columns(b)] + carried).astype(bf16)
        store(b).start()
    for b in range(NB):
        store(b).wait()


def whole(shape):
    return pl.BlockSpec(shape, lambda *g: (0,) * len(shape))


def params():
    return pltpu.CompilerParams(vmem_limit_bytes=16 << 20)


def cost(us):
    return pl.CostEstimate(flops=0, bytes_accessed=us * 3000000, transcendentals=0)


def local(x, dt, rate, in_map, out_map, gain):
    nz = lax.axis_size("d") // GROUP
    near = [[z * GROUP + p for p in range(GROUP)] for z in range(nz)]
    far = [[z * GROUP + p for z in range(nz)] for p in range(GROUP)]
    exchange = functools.partial(lax.all_to_all, axis_name="d", split_axis=0, concat_axis=0, tiled=True)
    dt, rate = dt.T, rate.T
    xspec = pl.BlockSpec((TOK, BPS * COLS), lambda g: (0, g))
    small = [whole((HEADS, TOK)), whole((HEADS, TOK)), whole((TOK, STATE))]
    matrix = pltpu.VMEM((TOK, 128), f32)
    hot = pltpu.VMEM((256, COLS), bf16)

    vmem, hbm = pl.BlockSpec(memory_space=pltpu.VMEM), pl.BlockSpec(memory_space=pl.ANY)
    sems = pltpu.SemaphoreType.DMA((NB,))
    sent = pl.pallas_call(
        state_kernel,
        in_specs=[pl.BlockSpec(memory_space=pltpu.HBM)] * 4,
        out_specs=vmem,
        out_shape=pltpu.VMEM((NA, NB, ROWS_S, 128), bf16),
        scratch_shapes=[
            pltpu.VMEM((NB, TOK, COLS), bf16),
            sems,
            pltpu.VMEM((HEADS, TOK), f32),
            pltpu.VMEM((STATE, TOK), f32),
            pltpu.VMEM((HEADS, TOK), bf16),
            pltpu.VMEM((HEADS, TOK), bf16),
            pltpu.VMEM((TOK, STATE), bf16),
            pltpu.SemaphoreType.DMA((3,)),
        ],
        compiler_params=pltpu.CompilerParams(vmem_limit_bytes=56 << 20),
        name="chunk_states",
    )(x, dt, rate, in_map)
    states = exchange(sent.reshape(GROUP, ROWS_S, 128), axis_index_groups=near)
    totals = pl.pallas_call(
        total_kernel,
        out_shape=pltpu.VMEM((nz, ROWS_S, 128), bf16),
        scratch_shapes=[pltpu.VMEM((GROUP * DEC, COLS), f32)],
        compiler_params=params(),
        name="block_total",
    )(states)
    totals = exchange(totals, axis_index_groups=far)
    gains = jnp.broadcast_to(jnp.pad(gain, (0, 128 - HEADS))[None, :], (8, 128))
    part, decay = pl.pallas_call(
        inner_kernel,
        grid=(STEPS,),
        in_specs=[xspec] + small + [whole((TOK, STATE)), whole((8, 128))],
        out_specs=[xspec, whole((TOK, 128))],
        out_shape=[pltpu.HBM(x.shape, f32), jax.ShapeDtypeStruct((TOK, 128), f32)],
        scratch_shapes=[matrix, matrix, pltpu.VMEM((TOK, TOK), bf16), hot],
        compiler_params=params(),
        cost_estimate=cost(4),
        name="inner_outputs",
    )(x, dt, rate, in_map, out_map, gains)
    entering = pl.pallas_call(
        enter_kernel,
        in_specs=[vmem, vmem, pl.BlockSpec(memory_space=pltpu.SMEM), hbm],
        out_specs=vmem,
        out_shape=pltpu.VMEM((GROUP, ROWS_H, 128), bf16),
        scratch_shapes=[
            pltpu.VMEM((GROUP * DEC, COLS), f32),
            pltpu.VMEM((nz * DEC, COLS), f32),
        ],
        compiler_params=params(),
        name="entering_states",
    )(states, totals, (lax.axis_index("d") // GROUP).astype(jnp.int32).reshape(1), decay)
    entering = exchange(entering, axis_index_groups=near).reshape(NA, NB, ROWS_H, 128)
    return pl.pallas_call(
        output_kernel,
        in_specs=[vmem, vmem, vmem, vmem],
        out_specs=hbm,
        out_shape=jax.ShapeDtypeStruct(x.shape, bf16),
        scratch_shapes=[
            pltpu.VMEM((NB, TOK, COLS), bf16),
            sems,
        ],
        compiler_params=params(),
        name="outputs",
    )(part, decay, out_map, entering)


def solution(mesh):
    line = Mesh(mesh.devices.reshape(-1), ("d",))
    split = P("d", None)
    return jax.shard_map(
        local,
        mesh=line,
        in_specs=(split, split, split, split, split, P()),
        out_specs=split,
        check_vma=False,
    )
```

```python
import functools

import jax
import jax.numpy as jnp
from jax import lax
from jax.experimental import pallas as pl
from jax.experimental.pallas import tpu as pltpu
from jax.sharding import Mesh
from jax.sharding import PartitionSpec as P

HEADS = 80
HEAD_DIM = 64
STATE = 128
TOK = 128
HB = 10
COLS = HB * HEAD_DIM
NB = HEADS // HB
NA = 8
ROWS = STATE // NA
TILES = COLS // 128
DEC = 8
STEPS = 4
BPS = NB // STEPS
GROUP = NA * NB
ROWS_H = TILES * ROWS
ROWS_S = ROWS_H + DEC

f32, bf16 = jnp.float32, jnp.bfloat16


def iota(shape, dim):
    return lax.broadcasted_iota(jnp.int32, shape, dim)


def dot(a, b):
    return jnp.dot(a, b, preferred_element_type=f32)


def one_hot():
    k, c = iota((256, COLS), 0), iota((256, COLS), 1)
    return ((k & 127) == (c >> 6)).astype(f32).astype(bf16)


def split2(v):
    hi = v.astype(bf16)
    lo = (v - hi.astype(f32)).astype(bf16)
    return jnp.concatenate([hi, lo], axis=1)


def across(matrix, heads_first):
    v = lax.dot_general(matrix, heads_first, (((1,), (1,)), ((), ())), preferred_element_type=f32)
    return jnp.concatenate([v, jnp.zeros((TOK, 128 - HEADS), f32)], axis=1)


def sums_and_steps(rate_ref, dt_ref):
    same = (iota((TOK, TOK), 0) == iota((TOK, TOK), 1)).astype(f32).astype(bf16)
    return across(triangle(), rate_ref[...]), across(same, dt_ref[...])


def triangle(upper=False):
    row, column = iota((TOK, TOK), 0), iota((TOK, TOK), 1)
    keep = row <= column if upper else row >= column
    return keep.astype(f32).astype(bf16)


def columns(b):
    return slice(b * COLS, (b + 1) * COLS)


def state_kernel(x_ref, dt_hbm, rate_hbm, in_hbm, out_ref, x_buf, x_sems, w_ref, bt_ref, dt_ref, rate_ref, in_ref, sems):
    def load(b):
        return pltpu.make_async_copy(x_ref.at[:, columns(b)], x_buf.at[b], x_sems.at[b])

    small = [
        pltpu.make_async_copy(src, dst, sems.at[i])
        for i, (src, dst) in enumerate([(rate_hbm, rate_ref), (dt_hbm, dt_ref), (in_hbm, in_ref)])
    ]
    for copy in small:
        copy.start()
    for b in range(NB):
        load(b).start()
    for copy in small:
        copy.wait()
    rate = rate_ref[...]
    c = dot(rate, triangle(upper=True))
    w_ref[...] = jnp.exp(c - c[:, TOK - 1:TOK]) * dt_ref[...].astype(f32)
    bt_ref[...] = in_ref[...].astype(f32).T
    total = lax.dot_general(
        jnp.ones((8, TOK), bf16), rate, (((1,), (1,)), ((), ())), preferred_element_type=f32)
    total = jnp.concatenate([total, jnp.zeros((8, 128 - HEADS), f32)], axis=1)
    left = iota((STATE, 128), 1) < HEAD_DIM
    lane = iota((8, 128), 1)
    for b in range(NB):
        load(b).wait()
    for b in range(NB):
        sums = pieces(pltpu.roll(total, (128 - HB * b) % 128, 1), lane)
        for j in range(TILES):
            h = b * HB + 2 * j
            rows = jnp.concatenate([bt_ref[...] * w_ref[h:h + 1, :], bt_ref[...] * w_ref[h + 1:h + 2, :]], axis=0)
            s = dot(rows.astype(bf16), x_buf[b, :, j * 128:(j + 1) * 128])
            s = jnp.where(left, s[:STATE], s[STATE:]).astype(bf16)
            for a in range(NA):
                out_ref[a, b, j * ROWS:(j + 1) * ROWS, :] = s[a * ROWS:(a + 1) * ROWS, :]
        for a in range(NA):
            out_ref[a, b, ROWS_H:ROWS_S, :] = sums


def pieces(total, lane):
    hi = total.astype(bf16).astype(f32)
    mid = (total - hi).astype(bf16).astype(f32)
    lo = total - hi - mid
    out = jnp.where(lane < HB, hi, 0.0)
    out = jnp.where((lane >= HB) & (lane < 2 * HB), pltpu.roll(mid, HB, 1), out)
    out = jnp.where((lane >= 2 * HB) & (lane < 3 * HB), pltpu.roll(lo, 2 * HB, 1), out)
    return out.astype(bf16)


def decays(ref, store):
    k, c = iota((128, COLS), 0), iota((128, COLS), 1)
    h = c >> 6
    spread = ((k == h) | (k == h + HB) | (k == h + 2 * HB)).astype(f32).astype(bf16)
    rows = ref[:, ROWS_H:ROWS_S, :].astype(f32).reshape(ref.shape[0] * DEC, 128).astype(bf16)
    store[...] = jnp.exp(-dot(rows, spread))
    return rows


def two(v):
    return jnp.concatenate([v, v], axis=0)


def zeros():
    return tuple(jnp.zeros((ROWS, 128), f32) for _ in range(TILES))


def follow(state, ref, at, dec_ref, row):
    rows = slice(row * 8, row * 8 + 8) if isinstance(row, int) else pl.ds(pl.multiple_of(row * 8, 8), 8)
    return tuple(
        state[j] * two(dec_ref[rows, j * 128:(j + 1) * 128]) + ref[at, j * ROWS:(j + 1) * ROWS, :].astype(f32)
        for j in range(TILES)
    )


def total_kernel(s_ref, out_ref, dec_ref):
    rows = decays(s_ref, dec_ref)
    sums = dot(jnp.full((8, GROUP * DEC), 1 / DEC, bf16), rows)
    sums = sums + pltpu.roll(sums, 128 - HB, 1) + pltpu.roll(sums, 128 - 2 * HB, 1)
    sums = pieces(sums, iota((8, 128), 1))
    total = lax.fori_loop(0, GROUP, lambda c, t: follow(t, s_ref, c, dec_ref, c), zeros(), unroll=8)
    for z in range(out_ref.shape[0]):
        for j in range(TILES):
            out_ref[z, j * ROWS:(j + 1) * ROWS, :] = total[j].astype(bf16)
        out_ref[z, ROWS_H:ROWS_S, :] = sums


def enter_kernel(s_ref, u_ref, z_ref, _, out_ref, dec_ref, udec_ref):
    decays(s_ref, dec_ref)
    decays(u_ref, udec_ref)
    mine = z_ref[0]
    state = zeros()
    for z in range(u_ref.shape[0] - 1):
        later = follow(state, u_ref, z, udec_ref, z)
        state = tuple(jnp.where(z < mine, new, old) for new, old in zip(later, state))

    def step(c, state):
        for j in range(TILES):
            out_ref[c, j * ROWS:(j + 1) * ROWS, :] = state[j].astype(bf16)
        return follow(state, s_ref, c, dec_ref, c)

    lax.fori_loop(0, GROUP, step, state, unroll=8)


def inner_kernel(x_ref, dt_ref, rate_ref, in_ref, map_ref, gain_ref, out_ref, done_ref, b_ref, a_ref, e_ref, g_ref, oh_ref):
    g = pl.program_id(0)

    @pl.when(g == 0)
    def _():
        c, dt = sums_and_steps(rate_ref, dt_ref)
        mid = c[TOK // 2 - 1:TOK // 2, :]
        b_ref[...] = jnp.exp(c - mid) * dt
        a_ref[...] = jnp.exp(mid - c)
        e_ref[...] = jnp.exp(-c)
        done_ref[...] = jnp.exp(-c[TOK - 8:, :])
        score = lax.dot_general(map_ref[...], in_ref[...], (((1,), (1,)), ((), ())), preferred_element_type=f32)
        g_ref[...] = jnp.where(iota((TOK, TOK), 0) >= iota((TOK, TOK), 1), score, 0.0).astype(bf16)
        oh_ref[...] = one_hot()

    for i in range(BPS):
        back = lax.rem(128 - HB * (g * BPS + i), 128)
        cols = slice(i * COLS, (i + 1) * COLS)
        x = x_ref[:, cols].astype(f32)
        oh = oh_ref[...]
        xs = (dot(split2(pltpu.roll(b_ref[...], back, 1)), oh) * x).astype(bf16)
        gain = dot(split2(pltpu.roll(gain_ref[...], back, 1)), oh)[0:1, :]
        weight = dot(split2(pltpu.roll(a_ref[...], back, 1)), oh)
        out_ref[0, :, cols] = gain * x + weight * dot(g_ref[...], xs)
        out_ref[1, :, cols] = dot(split2(pltpu.roll(e_ref[...], back, 1)), oh)


def output_kernel(part_ref, map_ref, h_ref, out_ref, out_buf, out_sems):
    def store(b):
        return pltpu.make_async_copy(out_buf.at[b], out_ref.at[:, columns(b)], out_sems.at[b])

    for b in range(NB):
        entering = jnp.concatenate(
            [
                jnp.concatenate([h_ref[a, b, j * ROWS:(j + 1) * ROWS, :] for a in range(NA)], axis=0)
                for j in range(TILES)
            ],
            axis=1,
        )
        carried = part_ref[1, :, columns(b)] * dot(map_ref[...], entering)
        out_buf[b] = (part_ref[0, :, columns(b)] + carried).astype(bf16)
        store(b).start()
    for b in range(NB):
        store(b).wait()


def whole(shape):
    return pl.BlockSpec(shape, lambda *g: (0,) * len(shape))


def params():
    return pltpu.CompilerParams(vmem_limit_bytes=16 << 20)


def cost(us):
    return pl.CostEstimate(flops=0, bytes_accessed=us * 3000000, transcendentals=0)


def local(x, dt, rate, in_map, out_map, gain):
    nz = lax.axis_size("d") // GROUP
    near = [[z * GROUP + p for p in range(GROUP)] for z in range(nz)]
    far = [[z * GROUP + p for z in range(nz)] for p in range(GROUP)]
    exchange = functools.partial(lax.all_to_all, axis_name="d", split_axis=0, concat_axis=0, tiled=True)
    dt, rate = dt.T, rate.T
    xspec = pl.BlockSpec((TOK, BPS * COLS), lambda g: (0, g))
    small = [whole((HEADS, TOK)), whole((HEADS, TOK)), whole((TOK, STATE))]
    matrix = pltpu.VMEM((TOK, 128), f32)
    hot = pltpu.VMEM((256, COLS), bf16)

    vmem, hbm = pl.BlockSpec(memory_space=pltpu.VMEM), pl.BlockSpec(memory_space=pl.ANY)
    sems = pltpu.SemaphoreType.DMA((NB,))
    sent = pl.pallas_call(
        state_kernel,
        in_specs=[pl.BlockSpec(memory_space=pltpu.HBM)] * 4,
        out_specs=vmem,
        out_shape=pltpu.VMEM((NA, NB, ROWS_S, 128), bf16),
        scratch_shapes=[
            pltpu.VMEM((NB, TOK, COLS), bf16),
            sems,
            pltpu.VMEM((HEADS, TOK), f32),
            pltpu.VMEM((STATE, TOK), f32),
            pltpu.VMEM((HEADS, TOK), bf16),
            pltpu.VMEM((HEADS, TOK), bf16),
            pltpu.VMEM((TOK, STATE), bf16),
            pltpu.SemaphoreType.DMA((3,)),
        ],
        compiler_params=pltpu.CompilerParams(vmem_limit_bytes=56 << 20),
        name="chunk_states",
    )(x, dt, rate, in_map)
    states = exchange(sent.reshape(GROUP, ROWS_S, 128), axis_index_groups=near)
    totals = pl.pallas_call(
        total_kernel,
        out_shape=pltpu.VMEM((nz, ROWS_S, 128), bf16),
        scratch_shapes=[pltpu.VMEM((GROUP * DEC, COLS), f32)],
        compiler_params=params(),
        name="block_total",
    )(states)
    totals = exchange(totals, axis_index_groups=far)
    gains = jnp.broadcast_to(jnp.pad(gain, (0, 128 - HEADS))[None, :], (8, 128))
    part, done = pl.pallas_call(
        inner_kernel,
        grid=(STEPS,),
        in_specs=[xspec] + small + [whole((TOK, STATE)), whole((8, 128))],
        out_specs=[pl.BlockSpec((2, TOK, BPS * COLS), lambda g: (0, 0, g)), whole((8, 128))],
        out_shape=[pltpu.HBM((2, *x.shape), f32), jax.ShapeDtypeStruct((8, 128), f32)],
        scratch_shapes=[matrix, matrix, matrix, pltpu.VMEM((TOK, TOK), bf16), hot],
        compiler_params=params(),
        cost_estimate=cost(4),
        name="inner_outputs",
    )(x, dt, rate, in_map, out_map, gains)
    entering = pl.pallas_call(
        enter_kernel,
        in_specs=[vmem, vmem, pl.BlockSpec(memory_space=pltpu.SMEM), hbm],
        out_specs=vmem,
        out_shape=pltpu.VMEM((GROUP, ROWS_H, 128), bf16),
        scratch_shapes=[
            pltpu.VMEM((GROUP * DEC, COLS), f32),
            pltpu.VMEM((nz * DEC, COLS), f32),
        ],
        compiler_params=params(),
        name="entering_states",
    )(states, totals, (lax.axis_index("d") // GROUP).astype(jnp.int32).reshape(1), done)
    entering = exchange(entering, axis_index_groups=near).reshape(NA, NB, ROWS_H, 128)
    return pl.pallas_call(
        output_kernel,
        in_specs=[vmem, vmem, vmem],
        out_specs=hbm,
        out_shape=jax.ShapeDtypeStruct(x.shape, bf16),
        scratch_shapes=[
            pltpu.VMEM((NB, TOK, COLS), bf16),
            sems,
        ],
        compiler_params=params(),
        name="outputs",
    )(part, out_map, entering)


def solution(mesh):
    line = Mesh(mesh.devices.reshape(-1), ("d",))
    split = P("d", None)
    return jax.shard_map(
        local,
        mesh=line,
        in_specs=(split, split, split, split, split, P()),
        out_specs=split,
        check_vma=False,
    )
```
